32 devices in a mesh: half: 2 (over x), dp: 8 (over z, core), mp: 2 (over y).
Axes of the slice: x: 2, y: 2, z: 4, core: 2. Of those that a mesh axis runs over, the one named last changes fastest.
Arguments:
- samples: bfloat16 [4, 16, 1024, 512], P(None, ('half', 'dp')), may hold values from -6 to 6
- seg_ids: int32 [4, 16, 1024], P(None, ('half', 'dp')), may hold values from 0 to 3, never falling along the last dimension, each value on 1 to 512 neighbouring positions
- data_ids: int32 [4, 16, 4], P(None, ('half', 'dp')), may hold values from 0 to 7, as said below
- test_rows: bfloat16 [4, 8192, 100], P(None, ('half', 'dp', 'mp')), may hold values from -6 to 6
- test_data: int32 [4, 8192], P(None, ('half', 'dp', 'mp')), may hold values from 0 to 7
- labels: int32 [4, 8192], P(None, ('half', 'dp', 'mp')), may hold values from 0 to 9
- norm_params: bfloat16 [4, 512], P(None, ('half', 'dp')), may hold values from -1.75 to 1.75
- w_qkv: bfloat16 [512, 3, 512], P(('half', 'dp'), None, 'mp'), may hold values from -0.25 to 0.25
- w_out: bfloat16 [512, 512], P('mp', ('half', 'dp')), may hold values from -2 to 2
- w_up: bfloat16 [512, 1024], P(('half', 'dp'), 'mp'), may hold values from -0.25 to 0.25
- w_down: bfloat16 [1024, 512], P('mp', ('half', 'dp')), may hold values from -0.1875 to 0.1875
- pool_value: bfloat16 [512, 512], P(('half', 'dp')), may hold values from -0.25 to 0.25
- pool_query: bfloat16 [4, 512], P(None, ('half', 'dp')), may hold values from -0.5 to 0.5
- w_dec: bfloat16 [512, 4032], replicated, may hold values from -0.15625 to 0.15625
- child_in: bfloat16 [32, 512], replicated, may hold values from -1 to 1
- child_out: bfloat16 [32, 512], replicated, may hold values from -0.25 to 0.25
Outputs:
- total_loss: float32 [], replicated
- grad_samples: float32 [4, 16, 1024, 512], P(None, ('half', 'dp'), 'mp')
- grad_norm_params: float32 [4, 512], P(None, ('half', 'dp'))
- grad_w_qkv: float32 [512, 3, 512], P(('half', 'dp'), None, 'mp')
- grad_w_out: float32 [512, 512], P('mp', ('half', 'dp'))
- grad_w_up: float32 [512, 1024], P(('half', 'dp'), 'mp')
- grad_w_down: float32 [1024, 512], P('mp', ('half', 'dp'))
- grad_pool_value: float32 [512, 512], P(('half', 'dp'))
- grad_pool_query: float32 [4, 512], P(None, ('half', 'dp'))
- grad_w_dec: float32 [512, 4032], replicated
- grad_child_in: float32 [32, 512], replicated
- grad_child_out: float32 [32, 512], replicated
The draws below stay inside these ranges and needn't reach their ends.
Inputs may be any that keep to these rules, and one draw needn't show every extreme that they name: `data_ids`: in every micro-batch, each dataset number of each half names some segment of that half's sequences, and the first segment of every sequence of one half has one dataset number.
All inputs are finite; a program needn't handle non-finite values.
Results may differ from the reference program's by a relative error of at most 0.029.
Values may be sent and summed in bfloat16 or wider, within the bound.
No kernel may reach another device: no remote copies, remote signals or barrier semaphores. Data moves between devices by JAX's collectives and lax.ppermute only.
A program may use at most 256 MiB of HBM per device.

```python
import math
import jax
import jax.numpy as jnp
import numpy as np
from jax import lax

D = 512
NH = 4
HD = 128
FF = 1024
F = 100
H = 512
C = 10
R = 32
E = 4032
LEN = 1024
MB = 4
NSEG = 4
NDS = 8
SEQS = 16
TROWS = 8192
QB = 512


def draw_data_ids(key, part):
    key = jax.random.fold_in(key, 7)
    key_star, key_rest, key_order = jax.random.split(key, 3)
    half_seqs = SEQS // 2
    slots = half_seqs * (NSEG - 1)
    star = jax.random.randint(key_star, (MB, 2, 1, 1), 0, NDS)
    rest = jax.random.randint(key_rest, (MB * 2, slots), 0, NDS)
    order_keys = jax.random.split(key_order, MB * 2)
    orders = jax.vmap(lambda one_key: jax.random.permutation(one_key, slots))(order_keys)
    ranks = jnp.argsort(orders, axis=1)
    rest = jnp.where(ranks < NDS, ranks, rest).astype(jnp.int32)
    rest = rest.reshape(MB, 2, half_seqs, NSEG - 1)
    merged = jnp.concatenate([jnp.broadcast_to(star, (MB, 2, half_seqs, 1)).astype(jnp.int32), rest], axis=3)
    return merged.reshape(MB, SEQS, NSEG).astype(jnp.int32)


def touch_ends(array, stream_key, smallest, top_value):
    place = [jax.random.randint(jax.random.fold_in(stream_key, axis), (), 0, length) for axis, length in enumerate(array.shape)]
    longest = array.shape.index(max(array.shape))
    neighbour = place[:longest] + [(place[longest] + 1) % array.shape[longest]] + place[longest + 1:]
    return array.at[tuple(place)].set(smallest).at[tuple(neighbour)].set(top_value)


def shard_levels(own_key, dims, cuts, low, largest):
    level = 1.0
    for dim, shards_of in cuts:
        draws = jax.random.uniform(jax.random.fold_in(jax.random.fold_in(own_key, 6), dim), (shards_of,), jnp.float32, low / len(cuts), largest / len(cuts))
        level = level * jnp.repeat(jnp.exp(draws), dims[dim] // shards_of).reshape((-1,) + (1,) * (len(dims) - 1 - dim))
    return level


def split_up(amount, total, reach, slope):
    portions = [(1 << 20) // math.isqrt(standing ** slope) + 1 for standing in range(2, amount + 1)]
    surplus, counts = total - reach - (amount - 1), [1] * (amount - 1)
    while surplus > 0:
        free = [i for i in range(amount - 1) if counts[i] < reach]
        mass, budget = sum([portions[i] for i in free]), surplus
        for i in free:
            more = min(reach - counts[i], max(1, budget * portions[i] // mass), surplus)
            counts[i] = counts[i] + more
            surplus = surplus - more
    return np.array([reach] + counts)


def ragged_sizes(rng, amount, total, reach, slope):
    if amount == 2:
        one = jax.random.randint(rng, (), max(1, total - reach), min(reach, total - 1) + 1)
        return jnp.stack([one, total - one])
    sizes = jnp.asarray(split_up(amount, total, reach, slope), jnp.int32)
    couples = (amount - 1) // 2
    source_of, receiver = sizes[1:1 + 2 * couples:2], sizes[2:2 + 2 * couples:2]
    room = jnp.minimum(source_of - 1, reach - receiver)
    moved = jax.random.randint(jax.random.fold_in(rng, 1), (couples,), 0, 1 << 20) % (room + 1)
    sizes = sizes.at[1:1 + 2 * couples:2].set(source_of - moved).at[2:2 + 2 * couples:2].set(receiver + moved)
    return sizes[jax.random.permutation(jax.random.fold_in(rng, 2), amount)]


def noise(stream_key, extent, scale, bound, cuts=(), dtype=jnp.bfloat16):
    loudness = shard_levels(stream_key, extent, cuts, -0.22, 0.18) if cuts else 1.0
    entries = jax.random.normal(stream_key, extent, jnp.float32) * scale * loudness
    return jnp.minimum(jnp.maximum(entries, -bound), bound).astype(dtype)


def setup_inputs(seed: int = 0) -> dict:
    key_list = jax.random.split(jax.random.key(seed), 17)
    samples = noise(key_list[0], (MB, SEQS, LEN, D), 1.0, 6.0, ((1, 16),))
    seg_ids = jax.vmap(lambda own: jnp.searchsorted(jnp.cumsum(ragged_sizes(own, NSEG, LEN, LEN // 2, 2)), jnp.arange(LEN), side="right"))(jax.random.split(key_list[1], MB * SEQS)).reshape((MB, SEQS, LEN)).astype(jnp.int32)
    data_ids = draw_data_ids(jax.random.fold_in(key_list[16], 71), 0)
    test_rows = noise(key_list[3], (MB, TROWS, F), 1.0, 6.0, ((1, 32),))
    test_data = touch_ends(jax.random.randint(key_list[4], (MB, TROWS), 0, NDS), jax.random.fold_in(key_list[4], 1), 0, NDS - 1).astype(jnp.int32)
    labels = touch_ends(jax.random.randint(key_list[5], (MB, TROWS), 0, C), jax.random.fold_in(key_list[5], 1), 0, C - 1).astype(jnp.int32)
    norm_params = noise(key_list[6], (4, D), 0.3, 1.75, ((1, 16),))
    w_qkv = noise(key_list[7], (D, 3, D), D ** -0.5, 0.25, ((0, 16), (2, 2)))
    w_out = noise(key_list[8], (D, D), (D // 64) ** -0.5, 2.0, ((0, 2), (1, 16)))
    w_up = noise(key_list[9], (D, FF), D ** -0.5, 0.25, ((0, 16), (1, 2)))
    w_down = noise(key_list[10], (FF, D), FF ** -0.5, 0.1875, ((0, 2), (1, 16)))
    pool_value = noise(key_list[11], (D, D), D ** -0.5, 0.25, ((0, 16),))
    pool_query = noise(key_list[12], (NH, D), (D // 4) ** -0.5, 0.5, ((1, 16),))
    w_dec = noise(key_list[13], (D, E), (3 * D) ** -0.5, 0.15625)
    child_in = noise(key_list[14], (R, H), R ** -0.5, 1.0)
    child_out = noise(key_list[15], (R, H), H ** -0.5, 0.25)
    return {"samples": samples, "seg_ids": seg_ids, "data_ids": data_ids, "test_rows": test_rows, "test_data": test_data, "labels": labels, "norm_params": norm_params, "w_qkv": w_qkv, "w_out": w_out, "w_up": w_up, "w_down": w_down, "pool_value": pool_value, "pool_query": pool_query, "w_dec": w_dec, "child_in": child_in, "child_out": child_out}


@jax.custom_vjp
def low(v):
    return lax.optimization_barrier(v.astype(jnp.bfloat16)).astype(jnp.float32)

@jax.custom_vjp
def low_back(v):
    return v

def low_keep(v):
    return (low(v), None)

def low_pass(kept, grad):
    return (grad,)

def back_keep(v):
    return (v, None)

def back_low(kept, grad):
    return (low(grad),)
low.defvjp(low_keep, low_pass)
low_back.defvjp(back_keep, back_low)
EPSILON = 1e-05
NEG_FILL = -1e+30
HIGHEST = lax.Precision.HIGHEST

def product(left, right):
    return jnp.dot(left, right, precision=HIGHEST, preferred_element_type=jnp.float32)

def layer_norm(values, gain_row, shift_row):
    center = values - lax.optimization_barrier(jnp.mean(values, -1, keepdims=True))
    spread = lax.optimization_barrier(jnp.mean(center * center, -1, keepdims=True))
    return center * lax.rsqrt(spread + EPSILON) * (1.0 + gain_row) + shift_row

def attend_rows(query_blk, seg_blk, key_all, value_all, seg_all):
    scores = jnp.einsum('hqe,hke->hqk', query_blk, key_all, precision=HIGHEST) / math.sqrt(HD)
    scores = low_back(scores)
    same_seg = seg_blk[:, None] == seg_all[None, :]
    scores = jnp.where(same_seg[None], scores, NEG_FILL)
    row_peak = lax.optimization_barrier(jnp.max(scores, -1, keepdims=True))
    exponent = jnp.exp(scores - row_peak)
    weights = low(exponent / lax.optimization_barrier(jnp.sum(exponent, -1, keepdims=True)))
    return jnp.einsum('hqk,hke->hqe', weights, value_all, precision=HIGHEST)

def encode(sequence, segments, params):
    norm_params, w_qkv, w_out, w_up, w_down = params
    projected = low(low_back(jnp.einsum('td,dcn->tcn', sequence, w_qkv, precision=HIGHEST)))
    split_heads = projected.reshape(LEN, 3, NH, HD).transpose(1, 2, 0, 3)
    block_count = LEN // QB
    query_blocks = split_heads[0].reshape(NH, block_count, QB, HD).transpose(1, 0, 2, 3)
    seg_blocks = segments.reshape(block_count, QB)

    def attend(block_pair):
        return jax.checkpoint(attend_rows)(block_pair[0], block_pair[1], split_heads[1], split_heads[2], segments)
    attended_output = lax.map(attend, (query_blocks, seg_blocks))
    attended_output = low(low_back(attended_output.transpose(0, 2, 1, 3).reshape(LEN, D)))
    attn_out = low_back(product(attended_output, w_out))
    first_norm = layer_norm(sequence + attn_out, norm_params[0], norm_params[1])
    upward_projected = low_back(product(low(first_norm), w_up))
    active_mask_rows = low(jax.nn.gelu(upward_projected, approximate=False))
    ffn_out = low_back(product(active_mask_rows, w_down))
    return layer_norm(first_norm + ffn_out, norm_params[2], norm_params[3])

def pool_half(encoded, segments, dataset_ids, pool_value, pool_query, w_dec):
    token_data = jnp.take_along_axis(dataset_ids, segments, axis=1).reshape(-1)
    flat_low = low(encoded.reshape(-1, D))
    pool_score = low_back(product(flat_low, pool_query.T))
    pool_val = low_back(product(flat_low, pool_value)).reshape(-1, NH, HD)
    member = token_data[:, None] == jnp.arange(NDS).astype(jnp.int32)[None, :]
    masked = jnp.where(member[:, :, None], pool_score[:, None, :], NEG_FILL)
    peak_all = lax.optimization_barrier(jnp.max(masked, 0))
    exponent = jnp.where(member[:, :, None], jnp.exp(masked - peak_all[None]), 0.0)
    weights = exponent / lax.optimization_barrier(jnp.sum(exponent, 0))[None]
    pooled = jnp.einsum('ndh,nhe->dhe', weights, pool_val, precision=HIGHEST).reshape(NDS, D)
    return low(low_back(product(low(pooled), w_dec)))

def child_loss(row_inputs, row_data, row_labels, coef_vals, child_in, child_out):
    selector = (row_data[:, None] == jnp.arange(NDS).astype(jnp.int32)[None, :]).astype(jnp.float32)
    first_part = coef_vals[:, :F * R].reshape(NDS, F, R)
    second_part = coef_vals[:, F * R:(F + C) * R].reshape(NDS, C * R)
    offsets = coef_vals[:, (F + C) * R:]
    projected = jnp.einsum('rf,dfk->rdk', row_inputs, first_part, precision=HIGHEST)
    reduced = low(jnp.einsum('rd,rdk->rk', selector, projected, precision=HIGHEST))
    before = product(reduced, child_in) + product(selector, offsets)
    hidden = low(jax.nn.gelu(before, approximate=False))
    narrow = product(hidden, child_out.T)
    picked = product(selector, second_part).reshape(-1, C, R)
    logits = jnp.einsum('rk,rck->rc', narrow, picked, precision=HIGHEST)
    row_peak = lax.optimization_barrier(jnp.max(logits, -1, keepdims=True))
    log_total = row_peak[:, 0] + jnp.log(lax.optimization_barrier(jnp.sum(jnp.exp(logits - row_peak), -1)))
    chosen = jnp.take_along_axis(logits, row_labels[:, None], axis=1)[:, 0]
    return jnp.sum(log_total - chosen)

def forward(samples, norm_params, w_qkv, w_out, w_up, w_down, pool_value, pool_query, w_dec, child_in, child_out, seg_ids, data_ids, test_rows, test_data, labels):
    params = (norm_params, w_qkv, w_out, w_up, w_down)
    half_seqs = SEQS // 2
    half_rows = TROWS // 2
    loss_total = jnp.zeros((), jnp.float32)
    for batch_idx in range(MB):
        encoded = lax.map(lambda seq_pair: encode(seq_pair[0], seq_pair[1], params), (samples[batch_idx], seg_ids[batch_idx]))
        coef_list = []
        for side in range(2):
            coef_list.append(pool_half(encoded[side * half_seqs:(side + 1) * half_seqs], seg_ids[batch_idx, side * half_seqs:(side + 1) * half_seqs], data_ids[batch_idx, side * half_seqs:(side + 1) * half_seqs], pool_value, pool_query, w_dec))
        for side in range(2):
            loss_total = loss_total + child_loss(test_rows[batch_idx, side * half_rows:(side + 1) * half_rows], test_data[batch_idx, side * half_rows:(side + 1) * half_rows], labels[batch_idx, side * half_rows:(side + 1) * half_rows], coef_list[1 - side], child_in, child_out)
    return loss_total / (MB * TROWS)

def reference(samples, seg_ids, data_ids, test_rows, test_data, labels, norm_params, w_qkv, w_out, w_up, w_down, pool_value, pool_query, w_dec, child_in, child_out):
    test_float = test_rows.astype(jnp.float32)

    def wrapped(samples_f, norms_f, qkv_f, out_f, up_f, down_f, pvalue_f, pquery_f, dec_f, cin_f, cout_f):
        return forward(samples_f, norms_f, qkv_f, out_f, up_f, down_f, pvalue_f, pquery_f, dec_f, cin_f, cout_f, seg_ids, data_ids, test_float, test_data, labels)
    total_loss, pullback = jax.vjp(wrapped, samples.astype(jnp.float32), norm_params.astype(jnp.float32), w_qkv.astype(jnp.float32), w_out.astype(jnp.float32), w_up.astype(jnp.float32), w_down.astype(jnp.float32), pool_value.astype(jnp.float32), pool_query.astype(jnp.float32), w_dec.astype(jnp.float32), child_in.astype(jnp.float32), child_out.astype(jnp.float32))
    grads = pullback(jnp.ones((), jnp.float32))
    return (total_loss, grads[0], grads[1], grads[2], grads[3], grads[4], grads[5], grads[6], grads[7], grads[8], grads[9], grads[10])
```

```python
import math

import jax
import jax.numpy as jnp
from jax import lax
from jax.sharding import PartitionSpec as P

NH = 4
HD = 128
F = 100
H = 512
C = 10
R = 32
NSEG = 4
NDS = 8


EPSILON = 1e-05
NEG_FILL = -1e30
HIGHEST = lax.Precision.HIGHEST
BF = jnp.bfloat16
F32 = jnp.float32


def dot(a, b, dims):
    return lax.dot_general(a, b, (dims, ((), ())), preferred_element_type=F32)


def swap(value, axis, bit):
    size = lax.axis_size(axis)
    return lax.ppermute(value, axis, [(i, i ^ (1 << bit)) for i in range(size)])


def bit_of(axis, bit):
    return lax.rem(lax.div(lax.axis_index(axis), 1 << bit), 2)


def ordered(mine, theirs, bit):
    low = jnp.where(bit == 0, mine, theirs)
    high = jnp.where(bit == 0, theirs, mine)
    return low, high


def hd_stages():
    count = lax.axis_size("dp").bit_length() - 1
    return [("dp", b) for b in range(count - 1, 0, -1)], ("half", 0), ("dp", 0)


def significance(stage):
    return 1000 if stage[0] == "half" else stage[1]


def gather_rows(value, stages):
    rows, cols = value.shape
    done = []
    for stage in stages:
        place = sum(significance(d) > significance(stage) for d in done)
        theirs = swap(value, *stage)
        value = jnp.stack(ordered(value, theirs, bit_of(*stage)), place)
        done.append(stage)
    return value.reshape(-1, cols)


def scatter_rows(value, stages, count):
    cols = value.shape[-1]
    left = sorted(stages, key=significance, reverse=True)
    value = value.reshape((2,) * len(left) + (value.shape[0] // count, cols))
    for stage in stages:
        place = left.index(stage)
        bit = bit_of(*stage)
        first = lax.index_in_dim(value, 0, place, False)
        second = lax.index_in_dim(value, 1, place, False)
        keep = jnp.where(bit == 0, first, second)
        give = jnp.where(bit == 0, second, first).astype(BF)
        value = keep + swap(give, *stage).astype(F32)
        left.remove(stage)
    return value


def sum_over(value, stages):
    for stage in stages:
        low, high = ordered(value, swap(value, *stage), bit_of(*stage))
        value = low + high
    return value


def combine_pools(earlier, later):
    peak_both = jnp.maximum(earlier[0], later[0])
    scale_one = jnp.exp(earlier[0] - peak_both)
    scale_two = jnp.exp(later[0] - peak_both)
    return (
        peak_both,
        earlier[1] * scale_one + later[1] * scale_two,
        earlier[2] * scale_one[..., None] + later[2] * scale_two[..., None],
    )


def normalise(values):
    center = values - jnp.mean(values, -1, keepdims=True)
    inverse = lax.rsqrt(jnp.mean(center * center, -1, keepdims=True) + EPSILON)
    return center * inverse, inverse


def normalise_back(grad, gain, scaled, inverse):
    inner = grad * (1.0 + gain)
    mean_one = jnp.mean(inner, -1, keepdims=True)
    mean_two = jnp.mean(inner * scaled, -1, keepdims=True)
    return inverse * (inner - mean_one - scaled * mean_two)


def gelu_both(values):
    cdf = 0.5 * (1.0 + lax.erf(values * math.sqrt(0.5)))
    density = jnp.exp(-0.5 * values * values) * (1.0 / math.sqrt(2.0 * math.pi))
    return values * cdf, cdf + values * density


def attend_forward(qkv, seg):
    batch, length = seg.shape
    heads = qkv.shape[-1] // (3 * HD)
    parts = qkv.reshape(batch, length, 3, heads, HD)

    def one(pair):
        part, row_seg = pair
        scores = jnp.einsum("qhe,khe->hqk", part[:, 0], part[:, 1], preferred_element_type=F32)
        scores = scores * (1.0 / math.sqrt(HD))
        scores = jnp.where((row_seg[:, None] == row_seg[None, :])[None], scores, NEG_FILL)
        peak = jnp.max(scores, -1, keepdims=True)
        shifted = jnp.exp(scores - peak)
        total = jnp.sum(shifted, -1, keepdims=True)
        out = jnp.einsum(
            "hqk,khe->qhe", (shifted / total).astype(BF), part[:, 2], preferred_element_type=F32
        )
        return out.astype(BF).reshape(length, heads * HD), (peak + jnp.log(total))[:, :, 0]

    outs, sums = lax.map(one, (parts, seg))
    return outs.reshape(batch * length, heads * HD), sums


def attend_backward(qkv, seg, grad, sums):
    batch, length = seg.shape
    heads = qkv.shape[-1] // (3 * HD)
    parts = qkv.reshape(batch, length, 3, heads, HD)
    grads = grad.reshape(batch, length, heads, HD)
    root = 1.0 / math.sqrt(HD)

    def one(group):
        part, row_seg, out_grad, log_sum = group
        query, key, value = part[:, 0], part[:, 1], part[:, 2]
        scores = jnp.einsum("qhe,khe->hqk", query, key, preferred_element_type=F32) * root
        same = (row_seg[:, None] == row_seg[None, :])[None]
        probs = jnp.where(same, jnp.exp(scores - log_sum[:, :, None]), 0.0)
        prob_grad = jnp.einsum("qhe,khe->hqk", out_grad, value, preferred_element_type=F32)
        inner = jnp.sum(probs * prob_grad, -1, keepdims=True)
        score_grad = (probs * (prob_grad - inner)).astype(BF)
        dq = jnp.einsum("hqk,khe->qhe", score_grad, key, preferred_element_type=F32) * root
        dk = jnp.einsum("hqk,qhe->khe", score_grad, query, preferred_element_type=F32) * root
        dv = jnp.einsum("hqk,qhe->khe", probs.astype(BF), out_grad, preferred_element_type=F32)
        return jnp.stack([dq, dk, dv], 1).astype(BF).reshape(length, 3 * heads * HD)

    return lax.map(one, (parts, seg, grads, sums)).reshape(batch * length, 3 * heads * HD)


def child_pass(row_inputs, row_data, row_labels, coef_low, in_weight, out_weight, row_total):
    row_count = row_inputs.shape[0]
    selector = (row_data[:, None] == jnp.arange(NDS, dtype=jnp.int32)[None, :]).astype(F32)
    first_cols = coef_low[:, : F * R].reshape(NDS, F, R).transpose(1, 0, 2).reshape(F, NDS * R)
    second_cols = coef_low[:, F * R : (F + C) * R].astype(F32)
    offsets = coef_low[:, (F + C) * R :].astype(F32)
    projected = jnp.dot(row_inputs, first_cols, preferred_element_type=F32)
    projected = projected.reshape(row_count, NDS, R)
    reduced_low = jnp.sum(selector[:, :, None] * projected, 1).astype(BF)
    before = jnp.dot(reduced_low, in_weight, preferred_element_type=F32) + jnp.dot(
        selector, offsets, precision=HIGHEST
    )
    hidden, slope = gelu_both(before)
    hidden_low = hidden.astype(BF)
    narrow = jnp.einsum("rh,kh->rk", hidden_low, out_weight, preferred_element_type=F32)
    picked = jnp.dot(selector, second_cols, precision=HIGHEST).reshape(row_count, C, R)
    logits = jnp.sum(narrow[:, None, :] * picked, -1)
    row_peak = jnp.max(logits, -1, keepdims=True)
    shifted = jnp.exp(logits - row_peak)
    row_sums = jnp.sum(shifted, -1, keepdims=True)
    target = (row_labels[:, None] == jnp.arange(C, dtype=jnp.int32)[None, :]).astype(F32)
    losses = row_peak[:, 0] + jnp.log(row_sums[:, 0]) - jnp.sum(logits * target, -1)
    loss_part = jnp.sum(losses) / row_total
    logit_grad = (shifted / row_sums - target) / row_total
    narrow_grad = jnp.sum(logit_grad[:, :, None] * picked, 1)
    picked_grad = (logit_grad[:, :, None] * narrow[:, None, :]).reshape(row_count, C * R)
    second_grad = jnp.dot(selector.T, picked_grad, precision=HIGHEST)
    hidden_grad = jnp.dot(narrow_grad, out_weight.astype(F32), precision=HIGHEST)
    out_part = jnp.dot(narrow_grad.T, hidden_low.astype(F32), precision=HIGHEST)
    before_grad = hidden_grad * slope
    offset_grad = jnp.dot(selector.T, before_grad, precision=HIGHEST)
    reduced_grad = jnp.dot(before_grad, in_weight.astype(F32).T, precision=HIGHEST)
    in_part = jnp.dot(reduced_low.astype(F32).T, before_grad, precision=HIGHEST)
    spread_grad = (selector[:, :, None] * reduced_grad[:, None, :]).reshape(row_count, NDS * R)
    first_grad = jnp.dot(row_inputs.astype(F32).T, spread_grad, precision=HIGHEST)
    first_grad = first_grad.reshape(F, NDS, R).transpose(1, 0, 2).reshape(NDS, F * R)
    coef_grad = jnp.concatenate([first_grad, second_grad, offset_grad], 1)
    return coef_grad, in_part, out_part, loss_part


def local(
    samples,
    seg_ids,
    data_ids,
    test_rows,
    test_data,
    labels,
    norm_params,
    w_qkv,
    w_out,
    w_up,
    w_down,
    pool_value,
    pool_query,
    w_dec,
    child_in,
    child_out,
):
    micro, seqs, length, width = samples.shape
    mp_size = lax.axis_size("mp")
    mp_index = lax.axis_index("mp")
    half_index = lax.axis_index("half")
    own = micro // mp_size
    shards = lax.axis_size("half") * lax.axis_size("dp")
    depth = w_qkv.shape[0]
    cols = w_qkv.shape[2]
    units = w_up.shape[1]
    row_total = micro * test_rows.shape[1] * shards * mp_size
    far, half_stage, core_stage = hd_stages()
    mp_stage = ("mp", 0)

    qkv_mine = gather_rows(w_qkv.reshape(depth, 3 * cols), far + [half_stage, core_stage])
    qkv_other = swap(qkv_mine, *mp_stage)
    extra = jnp.pad(jnp.concatenate([pool_query.T, norm_params.T], 1), ((0, 0), (0, 120)))
    shared = jnp.concatenate([w_out.T, w_up, w_down.T], 1)
    packed = jnp.concatenate([shared, swap(shared, *mp_stage), pool_value, extra], 1)
    packed = gather_rows(packed, [half_stage] + far + [core_stage])
    wide = cols + 2 * units

    def both(start, count):
        return jnp.concatenate(
            [packed[:, start : start + count], packed[:, wide + start : wide + start + count]], 1
        )

    out_t = both(0, cols)
    up_w = both(cols, units)
    down_t = both(cols + units, units)
    pvalue_w = packed[:, 2 * wide : 2 * wide + width]
    tail = packed[:, 2 * wide + width :].T
    pquery_w = tail[:NH]
    norms = tail[NH : NH + 4].astype(F32)

    start = mp_index * own
    tokens = lax.dynamic_slice_in_dim(samples, start, own, 0).reshape(own * seqs * length, width)
    seg = lax.dynamic_slice_in_dim(seg_ids, start, own, 0).reshape(own * seqs, length)
    seq_data = lax.dynamic_slice_in_dim(data_ids, start, own, 0).reshape(own * seqs, NSEG)
    qkv_a = dot(tokens, qkv_mine, ((1,), (0,))).astype(BF)
    heads_a, sums_a = attend_forward(qkv_a, seg)
    qkv_b = dot(tokens, qkv_other, ((1,), (0,))).astype(BF)
    heads_b, sums_b = attend_forward(qkv_b, seg)
    heads = jnp.concatenate([heads_a, heads_b], 1)
    attn = dot(heads, out_t, ((1,), (1,)))
    one_scaled, one_inverse = normalise(tokens.astype(F32) + attn)
    first = one_scaled * (1.0 + norms[0]) + norms[1]
    first_low = first.astype(BF)
    up = dot(first_low, up_w, ((1,), (0,)))
    act, slope = gelu_both(up)
    act = act.astype(BF)
    two_scaled, two_inverse = normalise(first + dot(act, down_t, ((1,), (1,))))
    enc_low = (two_scaled * (1.0 + norms[2]) + norms[3]).astype(BF)
    pool_val = dot(enc_low, pvalue_w, ((1,), (0,)))
    pool_score = dot(enc_low, pquery_w, ((1,), (1,)))

    token_data = jnp.zeros_like(seg)
    for segment in range(NSEG):
        token_data = jnp.where(seg == segment, seq_data[:, segment : segment + 1], token_data)
    member = token_data.reshape(own, seqs * length, 1) == jnp.arange(NDS, dtype=jnp.int32)
    member = member[..., None]
    scores = pool_score.reshape(own, seqs * length, 1, NH)
    vals = pool_val.reshape(own, seqs * length, NH, HD)
    masked = jnp.where(member, scores, NEG_FILL)
    peak = jnp.max(masked, 1)
    weight = jnp.where(member, jnp.exp(masked - peak[:, None]), 0.0)
    pools = (peak, jnp.sum(weight, 1), jnp.einsum("mndh,mnhe->mdhe", weight, vals))
    for stage in [core_stage] + far:
        theirs = jax.tree.map(lambda part: swap(part, *stage), pools)
        bit = bit_of(*stage)
        pairs = [ordered(a, b, bit) for a, b in zip(pools, theirs)]
        pools = combine_pools([p[0] for p in pairs], [p[1] for p in pairs])
    peak, total, accum = pools
    pooled = (accum / total[..., None]).reshape(own * NDS, width)
    pooled_low = pooled.astype(BF)

    def across(value, flip):
        pairs = [(i, i ^ flip) for i in range(2 * mp_size)]
        return lax.ppermute(value, ("half", "mp"), pairs)

    other_pooled = jnp.concatenate(
        ordered(across(pooled_low, mp_size), across(pooled_low, mp_size + 1), mp_index)
    )
    own_pooled = jnp.concatenate(ordered(pooled_low, across(pooled_low, 1), mp_index))
    coef = dot(other_pooled, w_dec, ((1,), (0,))).astype(BF).reshape(micro, NDS, -1)
    coef_grads, in_parts, out_parts, loss_parts = [], 0.0, 0.0, 0.0
    for m in range(micro):
        coef_part, in_part, out_part, loss_part = child_pass(
            test_rows[m], test_data[m], labels[m], coef[m], child_in, child_out, row_total
        )
        coef_grads.append(coef_part)
        in_parts = in_parts + in_part
        out_parts = out_parts + out_part
        loss_parts = loss_parts + loss_part
    coef_grad = jnp.concatenate(coef_grads, 0)

    part = dot(coef_grad.astype(BF), w_dec, ((1,), (1,)))
    low_part, high_part = part[: own * NDS], part[own * NDS :]
    same_mp = jnp.where(mp_index == 0, low_part, high_part)
    other_mp = jnp.where(mp_index == 0, high_part, low_part)
    pooled_grad = across(same_mp, mp_size) + across(other_mp, mp_size + 1)
    pooled_grad = sum_over(pooled_grad, [core_stage] + far)

    summed = lax.psum(
        jnp.concatenate([coef_grad.reshape(-1), in_parts.reshape(-1), out_parts.reshape(-1)]),
        ("dp", "mp"),
    )
    loss_sum = lax.psum(loss_parts, ("dp", "mp"))
    coef_size = coef_grad.size
    summed_coef = summed[:coef_size].reshape(coef_grad.shape).astype(BF)
    summed_child = summed[coef_size:].reshape(2, R, H)
    theirs_coef = swap(summed_coef, "half", 0)
    coef_all = jnp.concatenate(ordered(theirs_coef, summed_coef, half_index))
    pooled_all = jnp.concatenate(ordered(own_pooled, other_pooled, half_index))
    dec_grad = dot(pooled_all, coef_all, ((0,), (0,)))
    child_grad = summed_child + swap(summed_child, "half", 0)
    loss = loss_sum + swap(loss_sum, "half", 0)

    pooled_grad = pooled_grad.reshape(own, NDS, NH, HD)
    pool_w = jnp.where(member, jnp.exp(scores - peak[:, None]), 0.0) / total[:, None]
    val_grad = jnp.einsum("mndh,mdhe->mnhe", pool_w, pooled_grad).reshape(-1, width).astype(BF)
    weight_grad = jnp.einsum("mdhe,mnhe->mndh", pooled_grad, vals)
    centre = jnp.sum(pooled_grad * pooled.reshape(pooled_grad.shape), -1)
    score_grad = jnp.sum(pool_w * (weight_grad - centre[:, None]), 2).reshape(-1, NH).astype(BF)
    g_pvalue = dot(enc_low, val_grad, ((0,), (0,)))
    g_pquery = dot(enc_low, score_grad, ((0,), (0,)))
    enc_grad = dot(val_grad, pvalue_w, ((1,), (1,))) + dot(score_grad, pquery_w, ((1,), (0,)))
    g_gain_two = jnp.sum(enc_grad * two_scaled, 0)
    g_shift_two = jnp.sum(enc_grad, 0)
    second_grad = normalise_back(enc_grad, norms[2], two_scaled, two_inverse)
    ffn_grad = second_grad.astype(BF)
    g_down = dot(ffn_grad, act, ((0,), (0,)))
    up_grad = (dot(ffn_grad, down_t, ((1,), (0,))) * slope).astype(BF)
    g_up = dot(first_low, up_grad, ((0,), (0,)))
    first_grad = second_grad + dot(up_grad, up_w, ((1,), (1,)))
    g_gain_one = jnp.sum(first_grad * one_scaled, 0)
    g_shift_one = jnp.sum(first_grad, 0)
    input_grad = normalise_back(first_grad, norms[0], one_scaled, one_inverse)
    attn_grad = input_grad.astype(BF)
    g_out = dot(attn_grad, heads, ((0,), (0,)))
    heads_grad = dot(attn_grad, out_t, ((1,), (0,))).astype(BF)

    back_a = attend_backward(qkv_a, seg, heads_grad[:, :cols], sums_a)
    back_b = attend_backward(qkv_b, seg, heads_grad[:, cols:], sums_b)
    g_qkv_a = dot(tokens, back_a, ((0,), (0,)))
    g_qkv_b = dot(tokens, back_b, ((0,), (0,)))
    token_grad = (
        input_grad + dot(back_a, qkv_mine, ((1,), (1,))) + dot(back_b, qkv_other, ((1,), (1,)))
    )

    def give_mp(mine, other):
        return mine + swap(other.astype(BF), *mp_stage).astype(F32)

    order = [core_stage, half_stage] + far[::-1]
    early_mine = jnp.concatenate([g_out[:, :cols], g_up[:, :units], g_down[:, :units]], 1)
    early_other = jnp.concatenate([g_out[:, cols:], g_up[:, units:], g_down[:, units:]], 1)
    early = scatter_rows(give_mp(early_mine, early_other), order, shards)
    late = scatter_rows(give_mp(g_qkv_a, g_qkv_b), order, shards)
    norm_rows = jnp.stack([g_gain_one, g_shift_one, g_gain_two, g_shift_two], 1)
    small = jnp.concatenate([g_pvalue, g_pquery, norm_rows], 1)
    small = jnp.pad(small, ((0, 0), (0, 120)))
    small = scatter_rows(small, order, shards)
    small = small + swap(small, *mp_stage)

    token_grad = token_grad.reshape(own, seqs, mp_size, length // mp_size, width)
    keep = lax.dynamic_index_in_dim(token_grad, mp_index, 2, False)
    give = lax.dynamic_index_in_dim(token_grad, 1 - mp_index, 2, False).astype(BF)
    sample_grad = jnp.concatenate(ordered(keep, swap(give, *mp_stage).astype(F32), mp_index), 0)

    return (
        loss,
        sample_grad,
        small[:, width + NH : width + NH + 4].T,
        late.reshape(depth, 3, cols),
        early[:, :cols].T,
        early[:, cols : cols + units],
        early[:, cols + units :].T,
        small[:, :width],
        small[:, width : width + NH].T,
        dec_grad,
        child_grad[0],
        child_grad[1],
    )


def solution(mesh):
    placed = (
        P(None, ("half", "dp"), None, None),
        P(None, ("half", "dp"), None),
        P(None, ("half", "dp"), None),
        P(None, ("half", "dp", "mp"), None),
        P(None, ("half", "dp", "mp")),
        P(None, ("half", "dp", "mp")),
        P(None, ("half", "dp")),
        P(("half", "dp"), None, "mp"),
        P("mp", ("half", "dp")),
        P(("half", "dp"), "mp"),
        P("mp", ("half", "dp")),
        P(("half", "dp"), None),
        P(None, ("half", "dp")),
        P(),
        P(),
        P(),
    )
    return jax.shard_map(
        local,
        mesh=mesh,
        in_specs=placed,
        out_specs=(
            P(),
            P(None, ("half", "dp"), "mp", None),
            P(None, ("half", "dp")),
            P(("half", "dp"), None, "mp"),
            P("mp", ("half", "dp")),
            P(("half", "dp"), "mp"),
            P("mp", ("half", "dp")),
            P(("half", "dp"), None),
            P(None, ("half", "dp")),
            P(),
            P(),
            P(),
        ),
        check_vma=False,
    )
```

```python
import functools
import math

import jax
import jax.numpy as jnp
from jax import lax
from jax.experimental import pallas as pl
from jax.experimental.pallas import tpu as pltpu
from jax.sharding import PartitionSpec as P

NH = 4
HD = 128
F = 100
C = 10
R = 32
NSEG = 4
NDS = 8

EPSILON = 1e-05
NEG_FILL = -1e30
HIGHEST = lax.Precision.HIGHEST
BF = jnp.bfloat16
F32 = jnp.float32
VMEM_LIMIT = 56 * 1024 * 1024
TILE = 256
ROWS = 512

NN = ((1,), (0,))
NT = ((1,), (1,))
TN = ((0,), (0,))
ANY = pl.BlockSpec(memory_space=pl.ANY)


def dot(a, b, dims):
    return lax.dot_general(a, b, (dims, ((), ())), preferred_element_type=F32)


def cost(microseconds):
    return pl.CostEstimate(
        flops=int(microseconds * 1.15e9), bytes_accessed=1 << 20, transcendentals=0
    )


def params(*semantics):
    return pltpu.CompilerParams(dimension_semantics=semantics, vmem_limit_bytes=VMEM_LIMIT)


def whole(array):
    return pl.BlockSpec(array.shape, lambda *_: (0,) * array.ndim)


def struct(shape, dtype):
    return jax.ShapeDtypeStruct(shape, dtype)


def swap(value, axis, bit):
    size = lax.axis_size(axis)
    return lax.ppermute(value, axis, [(i, i ^ (1 << bit)) for i in range(size)])


def bit_of(axis, bit):
    return lax.rem(lax.div(lax.axis_index(axis), 1 << bit), 2)


def ordered(mine, theirs, bit):
    low = jnp.where(bit == 0, mine, theirs)
    high = jnp.where(bit == 0, theirs, mine)
    return low, high


def moved(stages):
    top = lax.axis_size("dp")
    flips = [top if axis == "half" else 1 << bit for axis, bit in stages]
    out = [0]
    for flip in flips:
        out = out + [p ^ flip for p in out]
    return out


def added(*values):
    total = values[0].astype(F32)
    for value in values[1:]:
        total = total + value.astype(F32)
    return total


def sum_over(value, stages):
    for stage in stages:
        value = value + swap(value, *stage)
    return value


INFO = 3


def info_kernel(batch, heading_ref, seg_ref, data_ref, info_ref, token_ref):
    micro, _, length = seg_ref.shape
    tiles = length // TILE
    for i in range(INFO):
        info_ref[i] = heading_ref[i]
    for m in range(batch):
        at = heading_ref[1] + m
        seg = seg_ref[at]
        data = data_ref[at]
        ends = [jnp.sum(jnp.where(seg < s, 1, 0)) for s in range(1, NSEG)]
        token = jnp.zeros_like(seg)
        for s in range(NSEG):
            token = jnp.where(seg == s, data[:, s:s + 1], token)
        token_ref[m] = token
        for t in range(tiles):
            low, high = jnp.int32(0), jnp.int32(length)
            for end in ends:
                low = jnp.where(end <= t * TILE, jnp.maximum(low, end), low)
                high = jnp.where(end >= (t + 1) * TILE, jnp.minimum(high, end), high)
            first = low // TILE
            count = jnp.maximum((high + TILE - 1) // TILE - first, min(2, tiles))
            place = INFO + m * tiles + t
            info_ref[place] = jnp.minimum(first, tiles - count)
            info_ref[place + batch * tiles] = count


def read_info(heading, seg_row, data_row, batch):
    length = seg_row.shape[-1]
    smem = pl.BlockSpec(memory_space=pltpu.SMEM)
    return pl.pallas_call(
        functools.partial(info_kernel, batch),
        in_specs=[smem, whole(seg_row), whole(data_row)],
        out_specs=[smem, pl.BlockSpec((batch, 1, length), lambda: (0, 0, 0))],
        out_shape=[struct((INFO + 2 * batch * (length // TILE),), jnp.int32),
                   struct((batch, 1, length), jnp.int32)],
        cost_estimate=cost(1.5),
        name="read_info",
    )(heading, seg_row, data_row)


def windows_of(info_ref, m, t, batch):
    tiles = pl.num_programs(1)
    place = INFO + m * tiles + t
    return info_ref[place], info_ref[place + batch * tiles]


def pack_first_kernel(out_ref, up_ref, down_ref, *refs):
    to_ref = refs[-1]
    cols, units = out_ref.shape[1], up_ref.shape[1]
    to_ref[:, :cols] = out_ref[...]
    to_ref[:, cols:cols + units] = up_ref[...]
    to_ref[:, cols + units:] = down_ref[...]


def pack_first(w_out, w_up, w_down, after=()):
    cols = w_out.shape[1] + w_up.shape[1] + w_down.shape[1]
    return pl.pallas_call(
        pack_first_kernel,
        in_specs=[whole(w) for w in (w_out, w_up, w_down)] + [ANY] * len(after),
        out_shape=struct((w_up.shape[0], cols), BF),
        cost_estimate=cost(1.5),
        name="pack_first",
    )(w_out, w_up, w_down, *after)


def pack_second_kernel(mine_ref, theirs_ref, value_ref, query_ref, norm_ref, *refs):
    to_ref = refs[-1]
    wide, width = mine_ref.shape[1], value_ref.shape[1]
    to_ref[:, :wide] = mine_ref[...]
    to_ref[:, wide:2 * wide] = theirs_ref[...]
    to_ref[:, 2 * wide:2 * wide + width] = value_ref[...]
    small = jnp.concatenate([query_ref[...].astype(F32), norm_ref[...].astype(F32),
                             jnp.zeros((HD - 8, to_ref.shape[0]), F32)], 0)
    to_ref[:, 2 * wide + width:] = small.T.astype(BF)


def pack_second(mine, theirs, pool_value, pool_query, norm_params, after=()):
    arrays = (mine, theirs, pool_value, pool_query, norm_params)
    return pl.pallas_call(
        pack_second_kernel,
        in_specs=[whole(a) for a in arrays] + [ANY] * len(after),
        out_shape=struct((mine.shape[0], 2 * mine.shape[1] + pool_value.shape[1] + HD), BF),
        cost_estimate=cost(1.5),
        name="pack_second",
    )(*arrays, *after)


def place_blocks(info_ref, from_ref, to_ref, flips):
    block = from_ref.shape[0] // len(flips)
    for p, flip in enumerate(flips):
        to = pl.multiple_of((info_ref[0] ^ flip) * block, block)
        to_ref[pl.ds(to, block), :] = from_ref[p * block:(p + 1) * block, :]


def as_column(row):
    return jnp.broadcast_to(row.astype(F32), (8, row.shape[1])).T


def attend_forward_kernel(heads, flips, batch, offset, info_ref, x_ref, shards_ref, row_ref, *refs):
    if offset:
        qkv_ref, heads_ref, e_ref, inv_ref, col_ref = refs[-5:]
        w_ref = shards_ref
    else:
        qkv_ref, heads_ref, e_ref, inv_ref, w_ref, col_ref = refs[-6:]
    m, t = pl.program_id(0), pl.program_id(1)
    width = heads * HD
    length = x_ref.shape[0]
    blocks = length // TILE

    if not offset:
        @pl.when((m == 0) & (t == 0))
        def _():
            place_blocks(info_ref, shards_ref, w_ref, flips)

    @pl.when(t == 0)
    def _():
        col_ref[...] = as_column(row_ref[0])
        scale = math.log2(math.e) / math.sqrt(HD)
        for r in range(0, length, TILE):
            full = dot(x_ref[r:r + TILE, :], w_ref[...], NN)
            qkv_ref[r:r + TILE, :width] = (full[:, :width] * scale).astype(BF)
            qkv_ref[r:r + TILE, width:] = full[:, width:].astype(BF)

    first, count = windows_of(info_ref, offset + m, t, batch)
    start = pl.multiple_of(first * TILE, TILE)
    here = pl.ds(pl.multiple_of(t * TILE, TILE), TILE)

    def attend(size):
        there = pl.ds(start, size)
        same = col_ref[here, 0:1] == row_ref[0, :, there].astype(F32)
        for h in range(heads):
            query = qkv_ref[here, h * HD:(h + 1) * HD]
            key = qkv_ref[there, width + h * HD:width + (h + 1) * HD]
            value = qkv_ref[there, 2 * width + h * HD:2 * width + (h + 1) * HD]
            scores = jnp.where(same, dot(query, key, NT), NEG_FILL)
            peak = jnp.max(scores, -1, keepdims=True)
            shifted = jnp.exp2(scores - peak)
            inverse = 1.0 / jnp.sum(shifted, -1, keepdims=True)
            low = shifted.astype(BF)
            e_ref[:, h * length:h * length + size] = low
            out = dot(low, value, NN) * inverse
            heads_ref[:, h * HD:(h + 1) * HD] = out.astype(BF)
            inv_ref[:, h:h + 1] = inverse

    for c in range(min(2, blocks), blocks + 1):
        pl.when(count == c)(functools.partial(attend, c * TILE))


def attend_forward(info, samples, shards, flips, seg_row, batch, part, before=None, after=()):
    length = seg_row.shape[-1]
    width, cols = samples.shape[1], shards.shape[1]
    heads = cols // (3 * HD)
    tiles = length // TILE
    total = batch * length
    offset, count = part
    tile = lambda m, t, *_: ((offset + m) * tiles + t, 0)
    outs = [struct((total, cols), BF), struct((total, heads * HD), BF),
            struct((total, heads * length), BF), struct((total, heads), F32)]
    out_specs = [
        pl.BlockSpec((length, cols), lambda m, t, *_: (offset + m, 0)),
        pl.BlockSpec((TILE, heads * HD), tile),
        pl.BlockSpec((TILE, heads * length), tile),
        pl.BlockSpec((TILE, heads), tile),
    ]
    inputs = [info, samples, shards, seg_row]
    aliases = {}
    if offset:
        aliases = {len(inputs) + i: i for i in range(len(outs))}
        inputs += list(before)
    else:
        outs += [struct(shards.shape, BF)]
        out_specs += [whole(shards)]
    inputs += list(after)
    return pl.pallas_call(
        functools.partial(attend_forward_kernel, heads, flips, batch, offset),
        grid_spec=pltpu.PrefetchScalarGridSpec(
            num_scalar_prefetch=1,
            grid=(count, tiles),
            in_specs=[
                pl.BlockSpec((length, width), lambda m, t, info: (info[1] + offset + m, 0)),
                whole(shards),
                pl.BlockSpec((1, 1, length), lambda m, t, info: (info[1] + offset + m, 0, 0)),
            ] + [ANY] * (len(inputs) - 4),
            out_specs=out_specs,
            scratch_shapes=[pltpu.VMEM((length, 8), F32)],
        ),
        out_shape=outs,
        input_output_aliases=aliases,
        compiler_params=params("arbitrary", "arbitrary"),
        cost_estimate=cost(7.5 * count),
        name="attend_forward",
    )(*inputs)


def attend_backward_kernel(heads, flips, batch, offset, final, last, info_ref, qkv_ref, grad_ref,
                           heads_ref, e_ref, inv_ref, x_ref, w_ref, *refs):
    refs = list(refs)
    dqkv, keys_acc, values_acc, weight_acc = refs[-4:]
    outs = refs[:-4]
    if last:
        other_ref, attn_ref = outs[:2]
        mine_ref, give_ref = outs[-2:]
        outs = outs[2:-2]
    else:
        tokens_ref = outs.pop()
    carry_ref = outs[0] if offset else None
    if final:
        keep_ref, send_ref = outs[-2:]
    else:
        total_ref = outs[-1]
    m, t = pl.program_id(0), pl.program_id(1)
    width = heads * HD
    length = qkv_ref.shape[0]
    blocks = length // TILE
    root = 1.0 / math.sqrt(HD)

    @pl.when(t == 0)
    def _():
        keys_acc[...] = jnp.zeros_like(keys_acc)
        values_acc[...] = jnp.zeros_like(values_acc)

    first, count = windows_of(info_ref, offset + m, t, batch)
    start = pl.multiple_of(first * TILE, TILE)
    here = pl.ds(pl.multiple_of(t * TILE, TILE), TILE)

    def attend(size):
        there = pl.ds(start, size)
        for h in range(heads):
            part = slice(h * HD, (h + 1) * HD)
            query = qkv_ref[here, part]
            key = qkv_ref[there, width + h * HD:width + (h + 1) * HD]
            value = qkv_ref[there, 2 * width + h * HD:2 * width + (h + 1) * HD]
            shifted = e_ref[:, h * length:h * length + size]
            grad = grad_ref[:, part].astype(F32) * inv_ref[:, h:h + 1]
            inner = jnp.sum(grad * heads_ref[:, part].astype(F32), -1, keepdims=True)
            grad = grad.astype(BF)
            score_grad = (shifted.astype(F32) * (dot(grad, value, NT) - inner)).astype(BF)
            dqkv[here, part] = (dot(score_grad, key, NN) * root).astype(BF)
            keys_acc[there, part] += dot(score_grad, query, TN)
            values_acc[there, part] += dot(shifted, grad, TN)

    for c in range(min(2, blocks), blocks + 1):
        pl.when(count == c)(functools.partial(attend, c * TILE))

    @pl.when(t == pl.num_programs(1) - 1)
    def _():
        dqkv[:, width:2 * width] = (keys_acc[...] * math.log(2.0)).astype(BF)
        dqkv[:, 2 * width:] = values_acc[...].astype(BF)
        weight = dot(x_ref[...], dqkv[...], TN)

        @pl.when(m == 0)
        def _():
            weight_acc[...] = weight + carry_ref[...] if offset else weight

        @pl.when(m != 0)
        def _():
            weight_acc[...] += weight

        if last:
            half = length // 2
            for ref, at in ((mine_ref, info_ref[2]), (give_ref, 1 - info_ref[2])):
                rows = pl.ds(pl.multiple_of(at * half, half), half)
                value = dot(dqkv[rows, :], w_ref[...], NT)
                value += other_ref[rows, :].astype(F32) + attn_ref[rows, :].astype(F32)
                ref[...] = value.astype(ref.dtype)
        else:
            tokens_ref[...] = dot(dqkv[...], w_ref[...], NT).astype(BF)

    @pl.when((m == pl.num_programs(0) - 1) & (t == pl.num_programs(1) - 1))
    def _():
        if final:
            take_blocks(info_ref, [(weight_acc, keep_ref, send_ref)], flips)
        else:
            total_ref[...] = weight_acc[...]


def take_blocks(info_ref, groups, flips):
    depth = groups[0][0].shape[0]
    block = depth // len(flips)
    for acc, keep_ref, send_ref in groups:
        if len(flips) == 1:
            keep_ref[...] = acc[:depth // 2, :].astype(BF)
            send_ref[...] = acc[depth // 2:, :].astype(BF)
            continue
        for p, flip in enumerate(flips):
            at = pl.multiple_of((info_ref[0] ^ flip) * block, block)
            ref = keep_ref if p < len(flips) // 2 else send_ref
            p = p % (len(flips) // 2)
            ref[p * block:(p + 1) * block, :] = acc[pl.ds(at, block), :].astype(BF)


def attend_backward(info, qkv, grad, which, heads_out, shifted, inverse, samples, weight, flips,
                    batch, part=None, rest=None, carry=None, after=()):
    total, cols = qkv.shape
    length = total // batch
    width = samples.shape[1]
    heads = cols // (3 * HD)
    tiles = length // TILE
    last = rest is not None
    offset, count = part or (0, batch)
    final = offset + count == batch
    tile = lambda m, t, *_: ((offset + m) * tiles + t, 0)
    sequence = lambda n: pl.BlockSpec((length, n), lambda m, t, *_: (offset + m, 0))
    if final:
        outs = [struct((width // 2, cols), BF)] * 2
    else:
        outs = [struct((width, cols), F32)]
    out_specs = [whole(o) for o in outs]
    if last:
        half = length // 2
        outs += [struct((count * half, width), F32), struct((count * half, width), BF)]
        out_specs += [pl.BlockSpec((half, width), lambda m, t, info: (m, 0))] * 2
    else:
        outs += [struct((total, width), BF)]
        out_specs += [sequence(width)]
    in_specs = [
        sequence(cols),
        pl.BlockSpec((TILE, heads * HD), lambda m, t, *_: ((offset + m) * tiles + t, which)),
        pl.BlockSpec((TILE, heads * HD), tile),
        pl.BlockSpec((TILE, heads * length), tile),
        pl.BlockSpec((TILE, heads), tile),
        pl.BlockSpec((length, width), lambda m, t, info: (info[1] + offset + m, 0)),
        whole(weight),
    ]
    inputs = [info, qkv, grad, heads_out, shifted, inverse, samples, weight]
    if last:
        in_specs += [sequence(width)] * 2
        inputs += list(rest)
    if offset:
        in_specs += [whole(carry)]
        inputs += [carry]
    return pl.pallas_call(
        functools.partial(attend_backward_kernel, heads, flips, batch, offset, final, last),
        grid_spec=pltpu.PrefetchScalarGridSpec(
            num_scalar_prefetch=1,
            grid=(count, tiles),
            in_specs=in_specs + [ANY] * len(after),
            out_specs=out_specs,
            scratch_shapes=[pltpu.VMEM((length, cols), BF), pltpu.VMEM((length, heads * HD), F32),
                            pltpu.VMEM((length, heads * HD), F32), pltpu.VMEM((width, cols), F32)],
        ),
        out_shape=outs,
        compiler_params=params("arbitrary", "arbitrary"),
        cost_estimate=cost(11.0 * count),
        name="attend_backward",
    )(*inputs, *after)


def normalise(values):
    center = values - jnp.mean(values, -1, keepdims=True)
    inverse = lax.rsqrt(jnp.mean(center * center, -1, keepdims=True) + EPSILON)
    return center * inverse, inverse


def normalise_back(grad, gain, scaled, inverse):
    inner = grad * gain
    mean_one = jnp.mean(inner, -1, keepdims=True)
    mean_two = jnp.mean(inner * scaled, -1, keepdims=True)
    return inverse * (inner - mean_one - scaled * mean_two)


def gelu_both(values):
    size = jnp.abs(values)
    t = 1.0 / (1.0 + (0.3275911 * math.sqrt(0.5)) * size)
    bell = jnp.exp(-0.5 * values * values)
    tail = 0.5 * 1.061405429
    for factor in (-1.453152027, 1.421413741, -0.284496736, 0.254829592):
        tail = tail * t + 0.5 * factor
    tail = tail * t * bell
    cdf = jnp.where(values >= 0.0, 1.0 - tail, tail)
    return values * cdf, cdf + values * bell * (1.0 / math.sqrt(2.0 * math.pi))


def encode_kernel(layout, flips, info_ref, x_ref, heads_a_ref, heads_b_ref, shards_ref, data_ref,
                  one_ref, one_inv_ref, act_ref, slope_ref, two_ref, two_inv_ref, vals_ref,
                  scores_ref, pool_ref, w_ref, tail_ref):
    m, t = pl.program_id(0), pl.program_id(1)
    width = x_ref.shape[1]
    half = heads_a_ref.shape[1]
    outs, ups, downs, value, extra = layout

    @pl.when((m == 0) & (t == 0))
    def _():
        place_blocks(info_ref, shards_ref, w_ref, flips)
        tail_ref[...] = w_ref[:, extra:extra + HD].astype(F32).T[:8]

    norms = tail_ref[NH:NH + 4, :]
    attn = dot(heads_a_ref[...], w_ref[:, outs[0]:outs[0] + half], NT)
    attn += dot(heads_b_ref[...], w_ref[:, outs[1]:outs[1] + half], NT)
    one, one_inverse = normalise(x_ref[...].astype(F32) + attn)
    one_ref[...] = one.astype(BF)
    one_inv_ref[...] = one_inverse
    total = one * (1.0 + norms[0:1]) + norms[1:2]
    low = total.astype(BF)
    units = act_ref.shape[1]
    step = 256
    for j in range(0, units, step):
        which, at = divmod(j, units // 2)
        act, slope = gelu_both(dot(low, w_ref[:, ups[which] + at:ups[which] + at + step], NN))
        act = act.astype(BF)
        act_ref[:, j:j + step] = act
        slope_ref[:, j:j + step] = slope.astype(BF)
        total += dot(act, w_ref[:, downs[which] + at:downs[which] + at + step], NT)
    two, two_inverse = normalise(total)
    two_ref[...] = two.astype(BF)
    two_inv_ref[...] = two_inverse
    enc = (two * (1.0 + norms[2:3]) + norms[3:4]).astype(BF)
    vals = dot(enc, w_ref[:, value:value + width], NN).astype(BF)
    vals_ref[...] = vals
    scores = dot(tail_ref[...].astype(BF), enc, NT)
    scores_ref[...] = scores
    member = data_ref[0] == lax.broadcasted_iota(jnp.int32, (NDS, x_ref.shape[0]), 0)

    @pl.when(t == 0)
    def _():
        pool_ref[:, :width] = jnp.zeros((NDS, width), F32)
        lane = lax.broadcasted_iota(jnp.int32, (NDS, pool_ref.shape[1] - width), 1)
        pool_ref[:, width:] = jnp.where(lane < NH, NEG_FILL, 0.0)

    for h in range(NH):
        part = slice(h * HD, (h + 1) * HD)
        masked = jnp.where(member, scores[h:h + 1], NEG_FILL)
        before = pool_ref[:, width + h:width + h + 1]
        peak = jnp.maximum(before, jnp.max(masked, -1, keepdims=True))
        weight = jnp.where(member, jnp.exp(masked - peak), 0.0)
        keep = jnp.exp(before - peak)
        count = slice(width + NH + h, width + NH + h + 1)
        pool_ref[:, count] = pool_ref[:, count] * keep + jnp.sum(weight, -1, keepdims=True)
        pool_ref[:, part] = pool_ref[:, part] * keep + dot(weight.astype(BF), vals[:, part], NN)
        pool_ref[:, width + h:width + h + 1] = peak


def encode(info, samples, heads_a, heads_b, shards, layout, flips, data_row, batch):
    total = heads_a.shape[0]
    width = samples.shape[1]
    units = 2 * width
    length = total // batch
    rows = min(ROWS, length)
    tiles = length // rows
    spec = lambda cols: pl.BlockSpec((rows, cols), lambda m, t, *_: (m * tiles + t, 0))
    shape = lambda cols, dtype: struct((total, cols), dtype)
    outs = [shape(width, BF), shape(1, F32), shape(units, BF), shape(units, BF), shape(width, BF),
            shape(1, F32), shape(width, BF), struct((8, total), F32),
            struct((batch * NDS, width + HD), F32), struct(shards.shape, BF),
            struct((8, width), F32)]
    return pl.pallas_call(
        functools.partial(encode_kernel, layout, flips),
        grid_spec=pltpu.PrefetchScalarGridSpec(
            num_scalar_prefetch=1,
            grid=(batch, tiles),
            in_specs=[
                pl.BlockSpec((rows, width), lambda m, t, info: ((info[1] + m) * tiles + t, 0)),
                spec(heads_a.shape[1]), spec(heads_b.shape[1]), whole(shards),
                pl.BlockSpec((1, 1, rows), lambda m, t, *_: (m, 0, t)),
            ],
            out_specs=[
                spec(width), spec(1), spec(units), spec(units), spec(width), spec(1), spec(width),
                pl.BlockSpec((8, rows), lambda m, t, *_: (0, m * tiles + t)),
                pl.BlockSpec((NDS, width + HD), lambda m, t, *_: (m, 0)),
                whole(shards), whole(outs[-1]),
            ],
        ),
        out_shape=outs,
        compiler_params=params("arbitrary", "arbitrary"),
        cost_estimate=cost(24.0),
        name="encode",
    )(info, samples, heads_a, heads_b, shards, data_row)


def encode_back_kernel(layout, flips, info_ref, one_ref, one_inv_ref, act_ref, slope_ref, two_ref,
                       two_inv_ref, vals_ref, scores_ref, heads_a_ref, heads_b_ref, data_ref,
                       pool_ref, grad_ref, w_ref, tail_ref, attn_ref, heads_ref, keep_a_ref,
                       send_a_ref, keep_b_ref, send_b_ref, acc_a, acc_b, value_acc, tail_acc):
    m, t = pl.program_id(0), pl.program_id(1)
    rows, width = one_ref.shape
    half = heads_a_ref.shape[1]
    units = act_ref.shape[1] // 2
    outs, ups, downs, value, extra = layout
    accs = (acc_a, acc_b)

    @pl.when((m == 0) & (t == 0))
    def _():
        for ref in (acc_a, acc_b, value_acc, tail_acc):
            ref[...] = jnp.zeros_like(ref)

    norms = tail_ref[NH:NH + 4, :]
    gain_one, gain_two = 1.0 + norms[0:1], 1.0 + norms[2:3]
    member = data_ref[0] == lax.broadcasted_iota(jnp.int32, (NDS, rows), 0)
    scores = scores_ref[...]
    val_grads, score_grads = [], []
    for h in range(NH):
        part = slice(h * HD, (h + 1) * HD)
        peak = pool_ref[:, width + h:width + h + 1]
        count = 1.0 / pool_ref[:, width + NH + h:width + NH + h + 1]
        masked = jnp.where(member, scores[h:h + 1], NEG_FILL)
        weight = jnp.where(member, jnp.exp(masked - peak), 0.0) * count
        pooled = pool_ref[:, part] * count
        grad = grad_ref[:, part].astype(BF)
        inner = dot(grad, vals_ref[:, part], NT)
        centre = jnp.sum(grad.astype(F32) * pooled, -1, keepdims=True)
        score_grads.append(jnp.sum(weight * (inner - centre), 0, keepdims=True))
        val_grads.append(dot(weight.astype(BF), grad, TN).astype(BF))
    val_grad = jnp.concatenate(val_grads, 1)
    zero = jnp.zeros_like(score_grads[0])
    score_grad = jnp.concatenate(score_grads + [zero] * 4, 0).astype(BF)
    two = two_ref[...].astype(F32)
    enc = (two * gain_two + norms[3:4]).astype(BF)
    value_acc[...] += dot(enc, val_grad, TN)
    enc_grad = dot(val_grad, w_ref[:, value:value + width], NT)
    enc_grad += dot(score_grad, tail_ref[...].astype(BF), TN)
    norm_grads = [None, None, jnp.sum(enc_grad * two, 0, keepdims=True),
                  jnp.sum(enc_grad, 0, keepdims=True)]
    two_grad = normalise_back(enc_grad, gain_two, two, two_inv_ref[...])
    ffn_grad = two_grad.astype(BF)
    one = one_ref[...].astype(F32)
    first = (one * gain_one + norms[1:2]).astype(BF)
    first_grad = two_grad
    for which in range(2):
        part = slice(which * units, (which + 1) * units)
        up, down = (slice(s[which], s[which] + units) for s in (ups, downs))
        up_grad = dot(ffn_grad, w_ref[:, down], NN) * slope_ref[:, part].astype(F32)
        up_grad = up_grad.astype(BF)
        accs[which][:, half + units:] += dot(ffn_grad, act_ref[:, part], TN)
        accs[which][:, half:half + units] += dot(first, up_grad, TN)
        first_grad += dot(up_grad, w_ref[:, up], NT)
    norm_grads[0] = jnp.sum(first_grad * one, 0, keepdims=True)
    norm_grads[1] = jnp.sum(first_grad, 0, keepdims=True)
    attn_grad = normalise_back(first_grad, gain_one, one, one_inv_ref[...]).astype(BF)
    attn_ref[...] = attn_grad
    for which, saved in enumerate((heads_a_ref, heads_b_ref)):
        part = slice(outs[which], outs[which] + half)
        heads_ref[:, which * half:(which + 1) * half] = dot(attn_grad, w_ref[:, part], NN).astype(BF)
        accs[which][:, :half] += dot(attn_grad, saved[...], TN)
    query_grad = dot(score_grad, enc, NN)
    tail_acc[:8] += jnp.concatenate([query_grad[:NH]] + norm_grads, 0)

    @pl.when((m == pl.num_programs(0) - 1) & (t == pl.num_programs(1) - 1))
    def _():
        end = half + 2 * units
        tail = tail_acc[...].T
        depth = tail.shape[0]
        block = depth // len(flips)
        for acc, keep_ref, send_ref in ((acc_a, keep_a_ref, send_a_ref),
                                        (acc_b, keep_b_ref, send_b_ref)):
            views = [keep_ref.at[:, :end], send_ref.at[:, :end]]
            take_blocks(info_ref, [(acc, *views)], flips)
            views = [keep_ref.at[:, end:end + width], send_ref.at[:, end:end + width]]
            take_blocks(info_ref, [(value_acc, *views)], flips)
        value_acc[:, :HD] = tail
        for keep_ref, send_ref in ((keep_a_ref, send_a_ref), (keep_b_ref, send_b_ref)):
            views = [keep_ref.at[:, end + width:], send_ref.at[:, end + width:]]
            take_blocks(info_ref, [(value_acc.at[:, :HD], *views)], flips)


def encode_back(info, saved, heads_a, heads_b, weights, tail, layout, flips, data_row, pool, grad,
                batch):
    one = saved[0]
    total, width = one.shape
    half = heads_a.shape[1]
    units = saved[2].shape[1]
    length = total // batch
    rows = min(ROWS, length)
    tiles = length // rows
    spec = lambda cols: pl.BlockSpec((rows, cols), lambda m, t, *_: (m * tiles + t, 0))
    cols = half + units + width + HD
    outs = [struct((total, width), BF)] * 2 + [struct((width // 2, cols), BF)] * 4
    return pl.pallas_call(
        functools.partial(encode_back_kernel, layout, flips),
        grid_spec=pltpu.PrefetchScalarGridSpec(
            num_scalar_prefetch=1,
            grid=(batch, tiles),
            in_specs=[
                spec(width), spec(1), spec(units), spec(units), spec(width), spec(1), spec(width),
                pl.BlockSpec((8, rows), lambda m, t, *_: (0, m * tiles + t)),
                spec(half), spec(half),
                pl.BlockSpec((1, 1, rows), lambda m, t, *_: (m, 0, t)),
                pl.BlockSpec((NDS, width + HD), lambda m, t, *_: (m, 0)),
                pl.BlockSpec((NDS, width), lambda m, t, *_: (m, 0)),
                whole(weights), whole(tail),
            ],
            out_specs=[spec(width), spec(width)] + [whole(o) for o in outs[2:]],
            scratch_shapes=[pltpu.VMEM((width, half + units), F32)] * 2
            + [pltpu.VMEM((width, width), F32), pltpu.VMEM((HD, width), F32)],
        ),
        out_shape=outs,
        compiler_params=params("arbitrary", "arbitrary"),
        cost_estimate=cost(27.0),
        name="encode_back",
    )(info, *saved, heads_a, heads_b, data_row, pool, grad, weights, tail)


def child_kernel(micro, row_total, info_ref, pooled_ref, dec_ref, rows_ref, data_ref, label_ref,
                 in_ref, out_ref, same_ref, other_ref, same_part_ref, other_part_ref, coef, coef_grad):
    hidden = in_ref.shape[1]
    group = HD // R
    chunks, classes = F // group, -(-C // group)
    second_start, bias_start = F * R, (F + C) * R
    coef[...] = dot(pooled_ref[...], dec_ref[...], NT).astype(BF).astype(F32)
    count = rows_ref.shape[-1]
    child_in, child_out = (jnp.concatenate([ref[...]] * group, 0) for ref in (in_ref, out_ref))
    spread_width = 256
    lanes = lax.broadcasted_iota(jnp.int32, (count, HD), 1)
    lane_data = lax.rem(lax.broadcasted_iota(jnp.int32, (count, group * spread_width), 1), NDS)
    lane_group = lanes // R
    lane_class = group * lax.rem(lanes // NDS, group) + lane_group
    row_group = lax.broadcasted_iota(jnp.int32, (NDS, HD), 1) // R
    place = lax.broadcasted_iota(jnp.int32, (F, group * spread_width), 1)
    inputs_of = group * (lax.rem(place, spread_width) // NDS) + place // spread_width
    expand = lax.broadcasted_iota(jnp.int32, (F, group * spread_width), 0) == inputs_of
    expand = jnp.where(expand, 1.0, 0.0).astype(BF)
    zeros = jnp.zeros((spread_width - chunks * NDS, HD), F32)
    inverse_total = 1.0 / row_total

    def one(m, carry):
        in_acc, out_acc, loss_acc = carry
        mine = pl.ds(pl.multiple_of(m * NDS, NDS), NDS)
        values = coef[mine, :]
        first = [values[:, c * HD:(c + 1) * HD] for c in range(chunks)]
        first = jnp.concatenate(first + [zeros], 0).astype(BF)
        second = []
        for g in range(group):
            for j in range(group):
                start = second_start + j * HD
                live = row_group == g
                if j < classes and group * j + g < C:
                    second.append(jnp.where(live, values[:, start:start + HD], 0.0))
                else:
                    second.append(jnp.zeros((NDS, HD), F32))
        second = jnp.concatenate(second, 0)
        bias = values[:, bias_start:].astype(BF)
        data, label = (as_column(ref[m])[:, :1].astype(jnp.int32) for ref in (data_ref, label_ref))
        spread = jnp.where(lane_data == data, dot(rows_ref[m], expand, TN), 0.0).astype(BF)
        reduced = jnp.zeros((count, HD), F32)
        for g in range(group):
            value = dot(spread[:, g * spread_width:(g + 1) * spread_width], first, NN)
            reduced = jnp.where(lane_group == g, value, reduced)
        reduced = reduced + pltpu.roll(reduced, 2 * R, 1)
        reduced = reduced + pltpu.roll(reduced, R, 1)
        reduced = jnp.where(lanes < R, reduced, 0.0).astype(BF)
        chosen = jnp.where(lanes[:, :NDS] == data, 1.0, 0.0).astype(BF)
        before = dot(reduced, child_in, NN) + dot(chosen, bias, NN)
        hid, slope = gelu_both(before)
        hid = hid.astype(BF)
        narrow = dot(hid, child_out, NT)
        logits = lax.dot_general(narrow, second, (NT, ((), ())), precision=HIGHEST,
                                 preferred_element_type=F32)
        live = (lax.rem(lanes, NDS) == data) & (lane_class < C)
        target = live & (lane_class == label)
        masked = jnp.where(live, logits, NEG_FILL)
        peak = jnp.max(masked, -1, keepdims=True)
        shifted = jnp.where(live, jnp.exp(masked - peak), 0.0)
        total = jnp.sum(shifted, -1, keepdims=True)
        picked = jnp.sum(jnp.where(target, logits, 0.0), -1, keepdims=True)
        losses = peak + jnp.log(total) - picked
        loss_acc = loss_acc + jnp.sum(losses, 0, keepdims=True) * inverse_total
        logit_grad = (shifted / total - jnp.where(target, 1.0, 0.0)) * inverse_total
        logit_grad = logit_grad.astype(BF)
        narrow_grad = dot(logit_grad, second.astype(BF), NN).astype(BF)
        second_grad = dot(logit_grad, narrow.astype(BF), TN)
        out_acc = out_acc + dot(narrow_grad, hid, TN)
        before_grad = (dot(narrow_grad, child_out, NN) * slope).astype(BF)
        bias_grad = dot(chosen, before_grad, TN)
        in_acc = in_acc + dot(reduced, before_grad, TN)
        reduced_grad = dot(before_grad, child_in, NT)
        first_grad = jnp.zeros((spread_width, HD), F32)
        for g in range(group):
            part = jnp.where(lane_group == g, reduced_grad, 0.0).astype(BF)
            first_grad += dot(spread[:, g * spread_width:(g + 1) * spread_width], part, TN)
        pieces = [first_grad[c * NDS:(c + 1) * NDS] for c in range(chunks)]
        for j in range(classes):
            piece = jnp.zeros((NDS, HD), F32)
            for g in range(group):
                at = (g * group + j) * NDS
                piece = jnp.where(row_group == g, second_grad[at:at + NDS], piece)
            pieces.append(piece[:, :min(HD, C * R - j * HD)])
        coef_grad[mine, :] = jnp.concatenate(pieces + [bias_grad], 1)
        return in_acc, out_acc, loss_acc

    zero = jnp.zeros((HD, hidden), F32)
    in_acc, out_acc, loss_acc = lax.fori_loop(0, micro, one, (zero, zero, jnp.zeros((1, 1), F32)))
    out_acc = sum(out_acc[g * R:(g + 1) * R] for g in range(group))
    rest = jnp.concatenate([in_acc[:R], out_acc, jnp.broadcast_to(loss_acc, (R, HD))], 1)
    parts = dot(coef_grad[...].astype(BF), dec_ref[...], NN)
    full = coef_grad.shape[1]
    rows = same_ref.shape[0]
    coef[:, :parts.shape[1]] = parts
    for ref, part_ref, at in ((same_ref, same_part_ref, info_ref[2]),
                              (other_ref, other_part_ref, 1 - info_ref[2])):
        place = pl.ds(pl.multiple_of(at * rows, rows), rows)
        ref[:, :full] = coef_grad[place, :].astype(BF)
        part_ref[...] = coef[place, :parts.shape[1]]
    rest = jnp.concatenate([rest[i * rows:(i + 1) * rows] for i in range(R // rows)], 1)
    same_ref[:, full:] = jnp.zeros((rows, same_ref.shape[1] - full), BF)
    same_ref[:, -rest.shape[1]:] = rest.astype(BF)


def child(info, pooled, dec, rows, data, label, child_in, child_out, micro, row_total, own):
    full = dec.shape[0]
    count = own * NDS
    wide = -(-full // HD) * HD + (R // count) * (2 * child_in.shape[1] + HD)
    width = pooled.shape[1]
    inputs = (pooled, dec, rows, data, label, child_in, child_out)
    return pl.pallas_call(
        functools.partial(child_kernel, micro, row_total),
        in_specs=[pl.BlockSpec(memory_space=pltpu.SMEM)] + [whole(a) for a in inputs],
        out_shape=[struct((count, wide), BF), struct((count, full), BF),
                   struct((count, width), F32), struct((count, width), F32)],
        scratch_shapes=[pltpu.VMEM((R, full), F32)] * 2,
        compiler_params=params(),
        cost_estimate=cost(16.0),
        name="child",
    )(info, *inputs)


def combine_kernel(bit_ref, mine_ref, theirs_ref, pool_ref, pooled_ref):
    width = pooled_ref.shape[1]
    swap_them = bit_ref[0] == 1
    mine, theirs = mine_ref[...], theirs_ref[...]
    low = jnp.where(swap_them, theirs, mine)
    high = jnp.where(swap_them, mine, theirs)
    for h in range(NH):
        part = slice(h * HD, (h + 1) * HD)
        at, count = slice(width + h, width + h + 1), slice(width + NH + h, width + NH + h + 1)
        peak = jnp.maximum(low[:, at], high[:, at])
        scale_low, scale_high = jnp.exp(low[:, at] - peak), jnp.exp(high[:, at] - peak)
        total = low[:, count] * scale_low + high[:, count] * scale_high
        accum = low[:, part] * scale_low + high[:, part] * scale_high
        pool_ref[:, part] = accum
        pool_ref[:, at] = peak
        pool_ref[:, count] = total
        pooled_ref[:, part] = (accum / total).astype(BF)
    pool_ref[:, width + 2 * NH:] = jnp.zeros_like(pool_ref[:, width + 2 * NH:])


def combine_pools(mine, theirs, bit):
    rows, cols = mine.shape
    return pl.pallas_call(
        combine_kernel,
        in_specs=[pl.BlockSpec(memory_space=pltpu.SMEM)] + [pl.BlockSpec(memory_space=pltpu.VMEM)] * 2,
        out_shape=[struct((rows, cols), F32),
                   struct((rows, cols - HD), BF)],
        cost_estimate=cost(1.5),
        name="combine_pools",
    )(bit.reshape(1), mine, theirs)


def local(
    samples,
    seg_ids,
    data_ids,
    test_rows,
    test_data,
    labels,
    norm_params,
    w_qkv,
    w_out,
    w_up,
    w_down,
    pool_value,
    pool_query,
    w_dec,
    child_in,
    child_out,
):
    micro, seqs, length, width = samples.shape
    mp_size = lax.axis_size("mp")
    mp_index = lax.axis_index("mp")
    half_index = lax.axis_index("half")
    own = micro // mp_size
    batch = own * seqs
    dp_size = lax.axis_size("dp")
    shards = lax.axis_size("half") * dp_size
    block = half_index * dp_size + lax.axis_index("dp")
    depth = w_qkv.shape[0]
    cols = w_qkv.shape[2]
    units = w_up.shape[1]
    hidden = child_in.shape[1]
    row_total = micro * test_rows.shape[1] * shards * mp_size
    far = [("dp", b) for b in range(dp_size.bit_length() - 2, 0, -1)]
    core_stage, half_stage, mp_stage = ("dp", 0), ("half", 0), ("mp", 0)

    gather_stages = far + [half_stage, core_stage]
    give_stages = [core_stage, half_stage] + far[::-1]
    gather_flips, give_flips = moved(gather_stages), moved(give_stages[::-1])
    direct = depth % 16 == 0
    one_block = [0]

    def doubled(value, stage):
        return jnp.concatenate([value, swap(value, *stage)], 0)

    def gathered(value):
        if direct:
            return value
        places = [gather_flips.index(flip) for flip in range(shards)]
        order = jnp.array(places, jnp.int32)[block ^ jnp.arange(shards, dtype=jnp.int32)]
        return value.reshape(shards, depth, -1)[order].reshape(value.shape)

    def in_turn(keep, send):
        if direct:
            return keep, send
        value = jnp.concatenate([keep, send], 0)
        order = block ^ jnp.array(give_flips, jnp.int32)
        value = value.reshape(shards, depth, -1)[order].reshape(value.shape)
        return value[: value.shape[0] // 2], value[value.shape[0] // 2 :]

    def halves(*values):
        rows = values[0].shape[0] // 2
        keep = added(*(v[:rows] for v in values))
        return keep, added(*(v[rows:] for v in values)).astype(BF)

    place_flips = gather_flips if direct else one_block
    take_flips = give_flips if direct else one_block

    qkv_steps = [w_qkv.reshape(depth, 3 * cols)]
    for stage in gather_stages:
        qkv_steps.append(doubled(qkv_steps[-1], stage))
    qkv_mine = qkv_steps[-1]
    if direct:
        shared = pack_first(w_out.T, w_up, w_down.T)
        packed = pack_second(
            shared, swap(shared, *mp_stage), pool_value, pool_query, norm_params,
            (qkv_steps[len(far)],),
        )
    else:
        extra = jnp.pad(jnp.concatenate([pool_query.T, norm_params.T], 1), ((0, 0), (0, HD - 8)))
        shared = jnp.concatenate([w_out.T, w_up, w_down.T], 1)
        packed = jnp.concatenate([shared, swap(shared, *mp_stage), pool_value, extra], 1)
    wide = shared.shape[1]
    layout = ((0, wide), (cols, wide + cols), (cols + units, wide + cols + units), 2 * wide,
              2 * wide + width)
    packed_start = packed
    *early_stages, z_stage, last_half, last_core = gather_stages
    for stage in early_stages:
        packed = doubled(packed, stage)

    start = mp_index * batch
    heading = jnp.stack([block if direct else block * 0, start, mp_index]).astype(jnp.int32)
    seg_row = seg_ids.reshape(-1, 1, length)
    info, token_data = read_info(heading, seg_row, data_ids.reshape(-1, 1, NSEG), batch)
    tokens = samples.reshape(-1, width)
    row_inputs = test_rows.transpose(0, 2, 1)
    row_data, row_labels = (ids.reshape(micro, 1, -1) for ids in (test_data, labels))

    def attend(shards, waits):
        *parts, full = attend_forward(
            info, tokens, shards, place_flips, seg_row, batch, (0, 1), after=waits[0]
        )
        if batch > 1:
            parts = attend_forward(
                info, tokens, full, place_flips, seg_row, batch, (1, batch - 1), parts, waits[1]
            )
        return *parts, full

    packed_z = doubled(packed, z_stage)
    qkv_other = swap(qkv_mine, *mp_stage)
    qkv_a, heads_a, shifted_a, inverse_a, full_a = attend(
        gathered(qkv_mine), ((row_data, row_labels, packed_start), (packed,))
    )
    packed_half = doubled(packed_z, last_half)
    qkv_b, heads_b, shifted_b, inverse_b, full_b = attend(
        gathered(qkv_other), ((heads_a, packed_z), ())
    )
    packed_half, heads_b = lax.optimization_barrier((packed_half, heads_b))
    packed = gathered(doubled(packed_half, last_core))
    *saved, pool, weights, tail = encode(
        info, tokens, heads_a, heads_b, packed, layout, place_flips, token_data, batch
    )
    for stage in [core_stage] + far:
        pool, pooled_low = combine_pools(pool, swap(pool, *stage), bit_of(*stage))

    def across(value, flip):
        pairs = [(i, i ^ flip) for i in range(2 * mp_size)]
        return lax.ppermute(value, ("half", "mp"), pairs)

    other_pooled = jnp.concatenate(
        ordered(across(pooled_low, mp_size), across(pooled_low, mp_size + 1), mp_index)
    )
    own_pooled = jnp.concatenate(ordered(pooled_low, across(pooled_low, 1), mp_index))
    coef_same, coef_other, part_same, part_other = child(
        info, other_pooled, w_dec.T, row_inputs, row_data, row_labels, child_in, child_out, micro,
        row_total, own,
    )

    full = w_dec.shape[1]
    pooled_grad = across(part_same, mp_size) + across(part_other, mp_size + 1)
    sums, from_other = across(coef_same, mp_size), across(coef_other, mp_size + 1)
    pooled_grad = sum_over(pooled_grad, [core_stage] + far)
    sums = jnp.concatenate(
        [added(sums[:, :full], from_other).astype(BF), sums[:, full:]], 1
    )
    pooled_grad, sums = lax.optimization_barrier((pooled_grad, sums))
    early_far, late_far = far[:1], far[1:]

    def summed(value, stages):
        for stage in stages:
            value = added(value, swap(value, *stage)).astype(BF)
        return value

    attn_grad, heads_grad, keep_a, send_a, keep_b, send_b = encode_back(
        info, saved, heads_a, heads_b, weights, tail, layout, take_flips, token_data, pool,
        pooled_grad, batch,
    )
    sums = summed(sums, early_far)
    sums, keep_a, send_a, keep_b, send_b = lax.optimization_barrier(
        (sums, keep_a, send_a, keep_b, send_b)
    )
    (keep_a, send_a), (keep_b, send_b) = in_turn(keep_a, send_a), in_turn(keep_b, send_b)
    sums = summed(sums, [core_stage])
    give = added(keep_b, swap(send_b, *core_stage)).astype(BF)
    mine = added(keep_a, swap(send_a, *core_stage)).astype(BF)
    early_mp = swap(give, *mp_stage)
    keep_o, send_o, rest = attend_backward(
        info, qkv_b, heads_grad, 1, heads_b, shifted_b, inverse_b, tokens, full_b, take_flips,
        batch, after=(give, mine, sums),
    )
    sums = summed(sums, late_far[:-1])
    sums_far = swap(sums, *late_far[-1])
    early_mp, sums_far, keep_o, send_o = lax.optimization_barrier(
        (early_mp, sums_far, keep_o, send_o)
    )
    sums = added(sums, sums_far).astype(BF)
    early_keep, early_send = halves(mine, early_mp)
    early = (early_keep, swap(early_send, *give_stages[1]))
    keep_o, send_o = in_turn(keep_o, send_o)
    late_give = added(keep_o, swap(send_o, *core_stage)).astype(BF)
    late_mp = swap(late_give, *mp_stage)
    sums_mp = swap(sums, *mp_stage)
    common = (info, qkv_a, heads_grad, 0, heads_a, shifted_a, inverse_a, tokens, full_a,
              take_flips, batch)
    waits = (early_keep, early_send, late_give)
    if batch > 1:
        carry, mine_first, give_first = attend_backward(
            *common, (0, batch - 1), (rest, attn_grad), after=waits
        )
        got_first = swap(give_first, *mp_stage)
        keep_m, send_m, mine_last, give_last = attend_backward(
            *common, (batch - 1, 1), (rest, attn_grad), carry
        )
    else:
        keep_m, send_m, mine_last, give_last = attend_backward(
            *common, None, (rest, attn_grad), after=waits
        )
        got_first, mine_first = give_last, mine_last
    keep_m, send_m, early, late_mp, got_first, sums_mp = lax.optimization_barrier(
        (keep_m, send_m, early, late_mp, got_first, sums_mp)
    )
    keep_m, send_m = in_turn(keep_m, send_m)
    late_keep, late_send = halves(keep_m, late_mp, swap(send_m, *core_stage))
    late_send, early, sums, sums_mp = lax.optimization_barrier((late_send, early, sums, sums_mp))
    got_last = swap(give_last, *mp_stage)
    steps = give_stages[1:]
    for i, stage in enumerate(steps):
        late = (late_keep, swap(late_send, *stage))
        if i < len(steps) - 1:
            early_keep, early_send = halves(*early)
            early = (early_keep, swap(early_send, *steps[i + 1]))
            late_keep, late_send = halves(*late)
        if i == 0:
            coef_half = jnp.concatenate(ordered(sums[:, :full], sums_mp[:, :full], mp_index))
            child_half = added(sums[:, full:], sums_mp[:, full:]).astype(BF)
            coef_rest, child_rest = swap(coef_half, "half", 0), swap(child_half, "half", 0)
        if i == len(steps) - 2:
            late_send, coef_rest, child_rest, got_last = lax.optimization_barrier(
                (late_send, coef_rest, child_rest, got_last)
            )
    coef_all = jnp.concatenate(ordered(coef_half, coef_rest, half_index))
    pooled_all = jnp.concatenate(ordered(own_pooled, other_pooled, half_index))
    dec_grad = dot(pooled_all, coef_all, TN)
    child_all = added(child_half, child_rest)
    child_cols = 2 * hidden + HD
    child_all = child_all[:, child_all.shape[1] - child_cols * (R // child_all.shape[0]) :]
    child_grad = jnp.concatenate(
        [child_all[:, at : at + child_cols] for at in range(0, child_all.shape[1], child_cols)]
    )

    own_grads, got_grads = [mine_last], [got_last]
    if batch > 1:
        own_grads, got_grads = [mine_first] + own_grads, [got_first] + got_grads
    pairs = [ordered(a, b.astype(F32), mp_index) for a, b in zip(own_grads, got_grads)]
    grads = jnp.concatenate([p[0] for p in pairs] + [p[1] for p in pairs])
    late, early = added(*late), added(*early)
    end = cols + 2 * units + width

    return (
        child_grad[0, 2 * hidden],
        grads.reshape(micro, seqs, length // mp_size, width),
        early[:, end + NH : end + NH + 4].T,
        late.reshape(depth, 3, cols),
        early[:, :cols].T,
        early[:, cols : cols + units],
        early[:, cols + units : cols + 2 * units].T,
        early[:, end - width : end],
        early[:, end : end + NH].T,
        dec_grad,
        child_grad[:, :hidden],
        child_grad[:, hidden : 2 * hidden],
    )


def solution(mesh):
    placed = (
        P(None, ("half", "dp"), None, None),
        P(None, ("half", "dp"), None),
        P(None, ("half", "dp"), None),
        P(None, ("half", "dp", "mp"), None),
        P(None, ("half", "dp", "mp")),
        P(None, ("half", "dp", "mp")),
        P(None, ("half", "dp")),
        P(("half", "dp"), None, "mp"),
        P("mp", ("half", "dp")),
        P(("half", "dp"), "mp"),
        P("mp", ("half", "dp")),
        P(("half", "dp"), None),
        P(None, ("half", "dp")),
        P(),
        P(),
        P(),
    )
    return jax.shard_map(
        local,
        mesh=mesh,
        in_specs=placed,
        out_specs=(
            P(),
            P(None, ("half", "dp"), "mp", None),
            P(None, ("half", "dp")),
            P(("half", "dp"), None, "mp"),
            P("mp", ("half", "dp")),
            P(("half", "dp"), "mp"),
            P("mp", ("half", "dp")),
            P(("half", "dp"), None),
            P(None, ("half", "dp")),
            P(),
            P(),
            P(),
        ),
        check_vma=False,
    )
```
